32 devices in a mesh: ctx: 8 (over y, x, core), ch: 4 (over z).
Axes of the slice: x: 2, y: 2, z: 4, core: 2. Of those that a mesh axis runs over, the one named last changes fastest.
Arguments:
- tokens: bfloat16 [3072, 4096], P('ctx', 'ch'), may hold values from -2.5 to 2.5
- mr_gain: float32 [4096], replicated, may hold values from 0.1 to 1.9
- mr_inproj: bfloat16 [4096, 3, 4096], P('ctx', None, 'ch'), may hold values from -0.09375 to 0.09375
- mr_outproj: bfloat16 [4096, 4096], P('ch', 'ctx'), may hold values from -0.09375 to 0.09375
- mr_filter: float32 [128, 4096], P(None, 'ch'), may hold values from -0.5 to 0.5
- li_gain: float32 [4096], replicated, may hold values from 0.1 to 1.9
- li_inproj: bfloat16 [4096, 3, 4096], P('ctx', None, 'ch'), may hold values from -0.09375 to 0.09375
- li_outproj: bfloat16 [4096, 4096], P('ch', 'ctx'), may hold values from -0.09375 to 0.09375
- li_decay: float32 [16, 4096], P(None, 'ch'), may hold values from 1.6276042e-06 to 0.125
- li_residue: float32 [16, 4096], P(None, 'ch'), may hold values from -1 to 1
- doc_ids: int32 [3072], replicated, may hold values from 0 to 3, never falling along the last dimension, each value on 1 to 1536 neighbouring positions
Outputs:
- layer_out: bfloat16 [3072, 4096], P('ctx', 'ch')
The draws below stay inside these ranges and needn't reach their ends.
Inputs may be any that keep to these rules, and one draw needn't show every extreme that they name: `doc_ids`: ids never fall along the sequence and every one of the 4 ids occurs.
All inputs are finite; a program needn't handle non-finite values.
Results may differ from the reference program's by a relative error of at most 0.03.
Values may be sent and summed in bfloat16 or wider, within the bound.
A program may use at most 192 MiB of HBM per device.

```python
import math
import jax
import jax.numpy as jnp
import numpy as np
from jax import lax

D = 4096
MODES = 16
MR_TAPS = 128
DOCS = 4
TOKENS = 3072
N_CTX = 8
N_CH = 4


def log_between(uniform_draw, lowest, highest):
    return jnp.exp(math.log(lowest) + uniform_draw * (math.log(highest) - math.log(lowest)))


def decay_rates(key):
    uniform_draw = jax.random.uniform(jax.random.fold_in(key, 101), (MODES, D), jnp.float32)
    return log_between(uniform_draw, min(2.0 / TOKENS, 1.0 / 64.0), 1.0 / 32.0)


def draw_li_decay(key, part):
    return decay_rates(key)


def draw_li_residue(key, part):
    rates = decay_rates(key)
    base_draw = jnp.clip(jax.random.normal(jax.random.fold_in(key, 202), (MODES, D), jnp.float32), -2.5, 2.5)
    scale = jnp.sqrt(jnp.maximum(2.0 * rates, 8.0 / TOKENS) / MODES) * 1.5
    return jnp.clip(base_draw * scale, -1.0, 1.0)


def level_of(own_key, extent, shards, low, high):
    loudness, own = 1.0, jax.random.fold_in(own_key, 6)
    for axis_at, blocks in shards:
        heights = jnp.exp(jax.random.uniform(jax.random.fold_in(own, axis_at), (blocks,), jnp.float32, low / len(shards), high / len(shards)))
        loudness = loudness * jnp.repeat(heights, extent[axis_at] // blocks).reshape([-1 if axis == axis_at else 1 for axis in range(len(extent))])
    return loudness


def length_profile(number_of, total, limit, skew):
    loads = [(1 << 20) // math.isqrt(standing ** skew) + 1 for standing in range(2, number_of + 1)]
    rest, given = total - limit - (number_of - 1), [1] * (number_of - 1)
    while rest > 0:
        candidates = [i for i in range(number_of - 1) if given[i] < limit]
        mass, left = sum([loads[i] for i in candidates]), rest
        for i in candidates:
            more = min(limit - given[i], max(1, left * loads[i] // mass), rest)
            given[i] = given[i] + more
            rest = rest - more
    return np.array([limit] + given)


def uneven_parts(rng, amount, total, reach, lean):
    if amount == 2:
        one = jax.random.randint(rng, (), max(1, total - reach), min(reach, total - 1) + 1)
        return jnp.stack([one, total - one])
    sizes = jnp.asarray(length_profile(amount, total, reach, lean), jnp.int32)
    twos = (amount - 1) // 2
    giver, receiver = sizes[1:1 + 2 * twos:2], sizes[2:2 + 2 * twos:2]
    room = jnp.minimum(giver - 1, reach - receiver)
    passed = jax.random.randint(jax.random.fold_in(rng, 1), (twos,), 0, 1 << 20) % (room + 1)
    sizes = sizes.at[1:1 + 2 * twos:2].set(giver - passed).at[2:2 + 2 * twos:2].set(receiver + passed)
    return sizes[jax.random.permutation(jax.random.fold_in(rng, 2), amount)]


def gaussian(stream_key, shape, scale, reach, shards=(), kind=jnp.bfloat16):
    values = scale * jax.random.normal(stream_key, shape, jnp.float32)
    if shards:
        values = values * level_of(stream_key, shape, shards, -0.22, 0.18)
    return jnp.clip(values, -reach, reach).astype(kind)


def setup_inputs(seed: int = 0) -> dict:
    splits = jax.random.split(jax.random.key(seed), 12)
    tokens = gaussian(splits[0], (TOKENS, D), 0.25, 2.5, ((0, 8), (1, 4)))
    mr_gain = jnp.clip(1.0 + 0.18 * jax.random.normal(splits[1], (D,), jnp.float32), 0.1, 1.9)
    mr_inproj = gaussian(splits[2], (D, 3, D), D ** -0.5, 0.09375, ((0, 8), (2, 4)))
    mr_outproj = gaussian(splits[3], (D, D), D ** -0.5, 0.09375, ((0, 4), (1, 8)))
    mr_filter = gaussian(splits[4], (MR_TAPS, D), MR_TAPS ** -0.5, 0.5, ((1, 4),), jnp.float32)
    li_gain = jnp.clip(1.0 + 0.18 * jax.random.normal(splits[5], (D,), jnp.float32), 0.1, 1.9)
    li_inproj = gaussian(splits[6], (D, 3, D), D ** -0.5, 0.09375, ((0, 8), (2, 4)))
    li_outproj = gaussian(splits[7], (D, D), D ** -0.5, 0.09375, ((0, 4), (1, 8)))
    li_decay = draw_li_decay(jax.random.fold_in(splits[11], 71), 0)
    li_residue = draw_li_residue(jax.random.fold_in(splits[11], 71), 0)
    doc_ids = jnp.searchsorted(jnp.cumsum(uneven_parts(splits[10], DOCS, TOKENS, TOKENS // 2, 2)), jnp.arange(TOKENS), side="right").astype(jnp.int32)
    return {"tokens": tokens, "mr_gain": mr_gain, "mr_inproj": mr_inproj, "mr_outproj": mr_outproj, "mr_filter": mr_filter, "li_gain": li_gain, "li_inproj": li_inproj, "li_outproj": li_outproj, "li_decay": li_decay, "li_residue": li_residue, "doc_ids": doc_ids}


def to_sequence(stored):
    blocks = stored.reshape((N_CTX, 2, stored.shape[0] // (2 * N_CTX)) + stored.shape[1:])
    return jnp.concatenate([blocks[:, 0], blocks[::-1, 1]], 0).reshape(stored.shape)

def to_stored(ordered):
    blocks = ordered.reshape((2 * N_CTX, ordered.shape[0] // (2 * N_CTX)) + ordered.shape[1:])
    return jnp.stack([blocks[:N_CTX], blocks[N_CTX:][::-1]], 1).reshape(ordered.shape)

def project_in(stream, gain, inproj):
    floats = stream.astype(jnp.float32)
    scaled = lax.rsqrt(lax.optimization_barrier(jnp.mean(floats * floats, axis=1, keepdims=True)) + 1e-06)
    normed = (floats * scaled * gain[None, :]).astype(jnp.bfloat16)
    joined = jnp.dot(normed, inproj.reshape(D, 3 * D), preferred_element_type=jnp.float32).astype(jnp.bfloat16)
    product = (joined[:, D:2 * D].astype(jnp.float32) * joined[:, 2 * D:].astype(jnp.float32)).astype(jnp.bfloat16)
    return (joined[:, :D], product)

def project_out(stream, query, mixed, outproj):
    gated = (query.astype(jnp.float32) * mixed).astype(jnp.bfloat16)
    group = D // N_CH

    def add_group(number, running):
        begin = (number * group).astype(jnp.int32)
        columns = lax.dynamic_slice_in_dim(gated, begin, group, 1)
        weights = lax.dynamic_slice_in_dim(outproj, begin, group, 0)
        partial_sum = jnp.dot(columns, weights, preferred_element_type=jnp.float32).astype(jnp.bfloat16)
        partial_sum = lax.optimization_barrier(partial_sum)
        return running + partial_sum.astype(jnp.float32)
    summed = lax.fori_loop(0, N_CH, add_group, jnp.zeros((TOKENS, D), jnp.float32))
    return (stream.astype(jnp.float32) + summed).astype(jnp.bfloat16)

def short_mix(product, mr_filter, doc_ids):
    floats = product.astype(jnp.float32)
    places = jnp.arange(TOKENS)

    def add_tap(tap_lag, running):
        moved = jnp.roll(floats, tap_lag, axis=0)
        moved_docs = jnp.roll(doc_ids, tap_lag)
        keep = (places >= tap_lag) & (moved_docs == doc_ids)
        weight = lax.dynamic_slice_in_dim(mr_filter, jnp.asarray(tap_lag).astype(jnp.int32), 1, 0)
        return running + jnp.where(keep[:, None], moved, 0.0) * weight
    return lax.fori_loop(0, MR_TAPS, add_tap, jnp.zeros((TOKENS, D), jnp.float32))

def combine_pairs(early, late):
    return (early[0] * late[0], late[0] * early[1] + late[1])

def long_mix(product, li_decay, li_residue, doc_ids):
    group = D // N_CH
    follows = jnp.concatenate([jnp.zeros((1,), bool), doc_ids[1:] == doc_ids[:-1]])

    def one_group(number):
        begin = (number * group).astype(jnp.int32)
        columns = lax.dynamic_slice_in_dim(product, begin, group, 1).astype(jnp.float32)
        rates = lax.dynamic_slice_in_dim(li_decay, begin, group, 1)
        weights = lax.dynamic_slice_in_dim(li_residue, begin, group, 1)
        carried = jnp.where(follows[:, None, None], jnp.exp(-rates)[None], 0.0)
        inputs = jnp.broadcast_to(columns[:, None, :], carried.shape)
        _, states = lax.associative_scan(combine_pairs, (carried, inputs), axis=0)
        return jnp.einsum('tmc,mc->tc', states, weights)
    parts = lax.map(one_group, jnp.arange(N_CH, dtype=jnp.int32))
    return jnp.transpose(parts, (1, 0, 2)).reshape(TOKENS, D)

def reference(tokens, mr_gain, mr_inproj, mr_outproj, mr_filter, li_gain, li_inproj, li_outproj, li_decay, li_residue, doc_ids):
    stream = to_sequence(tokens)
    query, product = project_in(stream, mr_gain, mr_inproj)
    stream = project_out(stream, query, short_mix(product, mr_filter, doc_ids), mr_outproj)
    query, product = project_in(stream, li_gain, li_inproj)
    stream = project_out(stream, query, long_mix(product, li_decay, li_residue, doc_ids), li_outproj)
    return to_stored(stream)
```

```python
import jax
import jax.numpy as jnp
from jax import lax
from jax.experimental import pallas as pl
from jax.experimental.pallas import tpu as pltpu
from jax.sharding import PartitionSpec as P

LANES = 128
ROWS = 8
VMEM_LIMIT = 40 * 1024 * 1024
vmem_spec = pl.BlockSpec(memory_space=pltpu.VMEM)
smem_spec = pl.BlockSpec(memory_space=pltpu.SMEM)


def gather_channels(stream):
    count, index = (lax.axis_size("ch"), lax.axis_index("ch"))
    channels = stream.shape[1]
    from_left, from_right = ([stream], [stream])
    for hop in range(1, count):
        up = [(i, i + 1) for i in range(hop - 1, count - 1)]
        down = [(i, i - 1) for i in range(1, count - hop + 1)]
        from_left.append(lax.ppermute(from_left[-1], "ch", up))
        from_right.append(lax.ppermute(from_right[-1], "ch", down))
    line = jnp.concatenate(from_left[:0:-1] + [stream] + from_right[1:], axis=1)
    return lax.dynamic_slice_in_dim(line, (count - 1 - index) * channels, count * channels, 1)


def scatter_channels(terms, stream):
    count, index = (lax.axis_size("ch"), lax.axis_index("ch"))
    channels = stream.shape[1]

    def block(number):
        begin = jnp.clip(number, 0, count - 1) * channels
        return lax.dynamic_slice_in_dim(terms, begin, channels, 1).astype(jnp.float32)

    total = block(index) + stream.astype(jnp.float32)
    right, left = (None, None)
    for far in range(count - 1, 0, -1):
        up = [(i, i + 1) for i in range(count - far)]
        down = [(i, i - 1) for i in range(far, count)]
        rightward, leftward = (block(index + far), block(index - far))
        if right is not None:
            rightward = rightward + right.astype(jnp.float32)
            leftward = leftward + left.astype(jnp.float32)
        right = lax.ppermute(rightward.astype(jnp.bfloat16), "ch", up)
        left = lax.ppermute(leftward.astype(jnp.bfloat16), "ch", down)
    return (total + right.astype(jnp.float32) + left.astype(jnp.float32)).astype(jnp.bfloat16)


def features_in(stream, gain, piece):
    whole = gather_channels(stream)
    floats = whole.astype(jnp.float32)
    scaled = lax.rsqrt(jnp.mean(floats * floats, axis=1, keepdims=True) + 1e-06)
    normed = (floats * scaled * gain[None, :]).astype(jnp.bfloat16)
    channels = piece.shape[2]
    flat = piece.reshape(piece.shape[0], 3 * channels)
    joined = jnp.dot(normed, flat, preferred_element_type=jnp.float32).astype(jnp.bfloat16)
    product = (
        joined[:, channels : 2 * channels].astype(jnp.float32)
        * joined[:, 2 * channels :].astype(jnp.float32)
    ).astype(jnp.bfloat16)
    return (joined[:, :channels], product)


def features_out(stream, query, mixed, piece):
    gated = (query.astype(jnp.float32) * mixed).astype(jnp.bfloat16)
    terms = jnp.dot(gated, piece, preferred_element_type=jnp.float32).astype(jnp.bfloat16)
    return scatter_channels(terms, stream)


def span_layout(shard_rows):
    ctx_count = lax.axis_size("ctx")
    ctx_index = lax.axis_index("ctx")
    span_rows = shard_rows // 2
    span_starts = jnp.stack([ctx_index * span_rows, (2 * ctx_count - 1 - ctx_index) * span_rows])
    return (ctx_count, ctx_index, span_rows, span_starts)


def short_kernel(docs, window, taps, out):
    span_rows = out.shape[1]
    reach = window.shape[1] - span_rows
    tile = out.shape[2:]

    def outputs(number, _):
        half = number // (span_rows // ROWS)
        row = pl.multiple_of((number % (span_rows // ROWS)) * ROWS, ROWS)
        first_doc = docs[half, reach + row]
        last_doc = docs[half, reach + row + ROWS - 1]

        def sources(step, sums):
            begin = row + step * ROWS
            base = reach - step * ROWS

            def load():
                source = [window[half, begin + b] for b in range(ROWS)]
                weight = [taps[base + d] for d in range(2 * ROWS - 1)]
                return source, weight

            def plain(sums):
                source, weight = load()
                sums = list(sums)
                for b in range(ROWS):
                    for a in range(ROWS):
                        sums[a] = sums[a] + source[b] * weight[a - b + ROWS - 1]
                return tuple(sums)

            def masked(sums):
                source, weight = load()
                sums = list(sums)
                for b in range(ROWS):
                    doc = docs[half, begin + b]
                    for a in range(ROWS):
                        same = jnp.where(doc == docs[half, reach + row + a], 1.0, 0.0)
                        sums[a] = sums[a] + (source[b] * same) * weight[a - b + ROWS - 1]
                return tuple(sums)

            return lax.cond(docs[half, begin] == last_doc, plain, masked, sums)

        def outside(step, skipped):
            return skipped + jnp.where(docs[half, row + step * ROWS + ROWS - 1] < first_doc, 1, 0)

        steps = reach // ROWS + 1
        skip = lax.fori_loop(0, steps, outside, jnp.int32(0))
        zero = jnp.zeros(tile, jnp.float32)
        sums = lax.fori_loop(skip, steps, sources, (zero,) * ROWS)
        for a in range(ROWS):
            out[half, row + a] = sums[a]
        return 0

    lax.fori_loop(0, 2 * (span_rows // ROWS), outputs, 0)


def short_mix(product, mr_filter, doc_ids):
    shard_rows, channels = product.shape
    ctx_count, ctx_index, span_rows, span_starts = span_layout(shard_rows)
    tap_count = mr_filter.shape[0]
    reach = -(-tap_count // ROWS) * ROWS
    halves = product.reshape(2, span_rows, channels)
    tails = halves[:, span_rows - reach :]
    up = [(i, i + 1) for i in range(ctx_count - 1)]
    down = [(i + 1, i) for i in range(ctx_count - 1)]
    before_lower = lax.ppermute(tails[0], "ctx", up)
    before_upper = lax.ppermute(tails[1], "ctx", down)
    before_upper = jnp.where(ctx_index == ctx_count - 1, tails[0], before_upper)
    window = jnp.concatenate([jnp.stack([before_lower, before_upper]), halves], 1)
    tile = (channels // LANES, LANES)
    window = window.astype(jnp.float32).reshape((2, reach + span_rows) + tile)
    places = span_starts[:, None] - reach + jnp.arange(reach + span_rows)[None, :]
    docs = jnp.where(places >= 0, jnp.take(doc_ids, jnp.clip(places, 0, None)), -1)
    taps = jnp.pad(mr_filter, ((ROWS - 1, reach + ROWS - tap_count), (0, 0)))
    taps = taps.reshape((taps.shape[0],) + tile)
    mixed = pl.pallas_call(
        short_kernel,
        out_shape=jax.ShapeDtypeStruct((2, span_rows) + tile, jnp.float32),
        in_specs=[smem_spec, vmem_spec, vmem_spec],
        out_specs=vmem_spec,
        compiler_params=pltpu.CompilerParams(vmem_limit_bytes=VMEM_LIMIT),
        cost_estimate=pl.CostEstimate(
            flops=2 * shard_rows * tap_count * channels,
            bytes_accessed=8 * shard_rows * channels,
            transcendentals=0,
        ),
        name="short_mix",
    )(docs, window, taps)
    return mixed.reshape(shard_rows, channels)


def states_kernel(follows, factor, values, finals):
    span_rows, modes = (values.shape[1], factor.shape[0])
    tile = values.shape[2:]
    for half in range(2):

        def step(row, states):
            value, keep = (values[half, row], follows[half, row])
            return tuple(states[m] * (factor[m] * keep) + value for m in range(modes))

        zero = jnp.zeros(tile, jnp.float32)
        states = lax.fori_loop(0, span_rows, step, (zero,) * modes)
        for m in range(modes):
            finals[half, m] = states[m]


def long_kernel(follows, factor, residue, initial, values, out):
    span_rows, modes = (values.shape[1], factor.shape[0])
    for half in range(2):

        def step(row, states):
            value, keep = (values[half, row], follows[half, row])
            states = tuple(states[m] * (factor[m] * keep) + value for m in range(modes))
            terms = [states[m] * residue[m] for m in range(modes)]
            while len(terms) > 1:
                pairs = [terms[k] + terms[k + 1] for k in range(0, len(terms) - 1, 2)]
                terms = pairs + terms[len(terms) - len(terms) % 2 :]
            out[half, row] = terms[0]
            return states

        lax.fori_loop(0, span_rows, step, tuple(initial[half, m] for m in range(modes)))


def long_mix(product, li_decay, li_residue, doc_ids):
    shard_rows, channels = product.shape
    ctx_count, ctx_index, span_rows, span_starts = span_layout(shard_rows)
    modes = li_decay.shape[0]
    tile = (channels // LANES, LANES)
    values = product.astype(jnp.float32).reshape((2, span_rows) + tile)
    decay = li_decay.reshape((modes,) + tile)
    residue = li_residue.reshape((modes,) + tile)
    factor = jnp.exp(-decay)
    places = span_starts[:, None] + jnp.arange(span_rows)[None, :]
    earlier = jnp.take(doc_ids, jnp.clip(places - 1, 0, None))
    follows = ((places > 0) & (jnp.take(doc_ids, places) == earlier)).astype(jnp.float32)
    params = pltpu.CompilerParams(vmem_limit_bytes=VMEM_LIMIT)
    flops = 2 * shard_rows * modes * channels
    finals = pl.pallas_call(
        states_kernel,
        out_shape=jax.ShapeDtypeStruct((2, modes) + tile, jnp.float32),
        in_specs=[smem_spec, vmem_spec, vmem_spec],
        out_specs=vmem_spec,
        compiler_params=params,
        cost_estimate=pl.CostEstimate(
            flops=flops, bytes_accessed=4 * shard_rows * channels, transcendentals=0
        ),
        name="block_states",
    )(follows, factor, values)
    before_docs = earlier[:, 0]
    initial = jnp.zeros((2, modes) + tile, jnp.float32)
    for shift in range(ctx_count):
        source = (ctx_index - shift) % ctx_count
        states = finals
        if shift:
            ring = [(i, (i + shift) % ctx_count) for i in range(ctx_count)]
            states = lax.ppermute(finals, "ctx", ring)
        for part, block in enumerate((source, 2 * ctx_count - 1 - source)):
            last = (block + 1) * span_rows - 1
            gap = span_starts - 1 - last
            keep = (gap >= 0) & (jnp.take(doc_ids, last) == before_docs)
            distance = jnp.where(keep, gap, 0).astype(jnp.float32)[:, None, None, None]
            weight = jnp.exp(-decay[None] * distance) * keep.astype(jnp.float32)[:, None, None, None]
            initial = initial + weight * states[part][None]
    mixed = pl.pallas_call(
        long_kernel,
        out_shape=jax.ShapeDtypeStruct((2, span_rows) + tile, jnp.float32),
        in_specs=[smem_spec] + [vmem_spec] * 4,
        out_specs=vmem_spec,
        compiler_params=params,
        cost_estimate=pl.CostEstimate(
            flops=2 * flops, bytes_accessed=8 * shard_rows * channels, transcendentals=0
        ),
        name="long_mix",
    )(follows, factor, residue, initial, values)
    return mixed.reshape(shard_rows, channels)


def body(
    tokens,
    mr_gain,
    mr_inproj,
    mr_outproj,
    mr_filter,
    li_gain,
    li_inproj,
    li_outproj,
    li_decay,
    li_residue,
    doc_ids,
):
    mr_in = lax.all_gather(mr_inproj, "ctx", axis=0, tiled=True)
    mr_out = lax.all_gather(mr_outproj, "ctx", axis=1, tiled=True)
    li_in = lax.all_gather(li_inproj, "ctx", axis=0, tiled=True)
    li_out = lax.all_gather(li_outproj, "ctx", axis=1, tiled=True)
    query, product = features_in(tokens, mr_gain, mr_in)
    stream = features_out(tokens, query, short_mix(product, mr_filter, doc_ids), mr_out)
    query, product = features_in(stream, li_gain, li_in)
    return features_out(stream, query, long_mix(product, li_decay, li_residue, doc_ids), li_out)


def solution(mesh):
    in_specs = (
        P("ctx", "ch"),
        P(),
        P("ctx", None, "ch"),
        P("ch", "ctx"),
        P(None, "ch"),
        P(),
        P("ctx", None, "ch"),
        P("ch", "ctx"),
        P(None, "ch"),
        P(None, "ch"),
        P(),
    )
    out_specs = P("ctx", "ch")
    return jax.shard_map(body, mesh=mesh, in_specs=in_specs, out_specs=out_specs, check_vma=False)
```

```python
import jax
import jax.numpy as jnp
from jax import lax
from jax.experimental import pallas as pl
from jax.experimental.pallas import tpu as pltpu
from jax.sharding import PartitionSpec as P

LANES = 128
ROWS = 8
VMEM_LIMIT = 40 * 1024 * 1024
vmem_spec = pl.BlockSpec(memory_space=pltpu.VMEM)
smem_spec = pl.BlockSpec(memory_space=pltpu.SMEM)


def gather_channels(stream):
    count, index = (lax.axis_size("ch"), lax.axis_index("ch"))
    channels = stream.shape[1]
    from_left, from_right = ([stream], [stream])
    for hop in range(1, count):
        up = [(i, i + 1) for i in range(hop - 1, count - 1)]
        down = [(i, i - 1) for i in range(1, count - hop + 1)]
        from_left.append(lax.ppermute(from_left[-1], "ch", up))
        from_right.append(lax.ppermute(from_right[-1], "ch", down))
    line = jnp.concatenate(from_left[:0:-1] + [stream] + from_right[1:], axis=1)
    return lax.dynamic_slice_in_dim(line, (count - 1 - index) * channels, count * channels, 1)


def scatter_channels(terms, streams):
    count, index = (lax.axis_size("ch"), lax.axis_index("ch"))
    rows, channels = streams[0].shape
    parts = range(len(streams))

    def block(part, number):
        begin = jnp.clip(number, 0, count - 1) * channels
        own = terms[part * rows : (part + 1) * rows]
        return lax.dynamic_slice_in_dim(own, begin, channels, 1).astype(jnp.float32)

    right, left = ([None for _ in parts], [None for _ in parts])
    for far in range(count - 1, 0, -1):
        up = [(i, i + 1) for i in range(count - far)]
        down = [(i, i - 1) for i in range(far, count)]
        for part in parts:
            rightward, leftward = (block(part, index + far), block(part, index - far))
            if right[part] is not None:
                rightward = rightward + right[part].astype(jnp.float32)
                leftward = leftward + left[part].astype(jnp.float32)
            right[part] = lax.ppermute(rightward.astype(jnp.bfloat16), "ch", up)
            left[part] = lax.ppermute(leftward.astype(jnp.bfloat16), "ch", down)
    summed = []
    for part in parts:
        total = block(part, index) + streams[part].astype(jnp.float32)
        total = total + right[part].astype(jnp.float32) + left[part].astype(jnp.float32)
        summed.append(total.astype(jnp.bfloat16))
    return summed


def features_in(streams, gain, piece, early):
    whole = jnp.concatenate([gather_channels(part) for part in streams], axis=0)
    floats = whole.astype(jnp.float32)
    scaled = lax.rsqrt(jnp.mean(floats * floats, axis=1, keepdims=True) + 1e-06)
    if early is not None:
        scaled, early = lax.optimization_barrier((scaled, early))
    normed = (floats * scaled * gain[None, :]).astype(jnp.bfloat16)
    channels = piece.shape[2]
    flat = piece.reshape(piece.shape[0], 3 * channels)
    joined = jnp.dot(normed, flat, preferred_element_type=jnp.float32).astype(jnp.bfloat16)
    product = (
        joined[:, channels : 2 * channels].astype(jnp.float32)
        * joined[:, 2 * channels :].astype(jnp.float32)
    ).astype(jnp.bfloat16)
    return (joined[:, :channels], product, early)


def features_out(streams, query, mixed, piece):
    gated = (query.astype(jnp.float32) * mixed).astype(jnp.bfloat16)
    terms = jnp.dot(gated, piece, preferred_element_type=jnp.float32).astype(jnp.bfloat16)
    return scatter_channels(terms, streams)


def span_layout(shard_rows):
    ctx_count = lax.axis_size("ctx")
    ctx_index = lax.axis_index("ctx")
    span_rows = shard_rows // 2
    span_starts = jnp.stack([ctx_index * span_rows, (2 * ctx_count - 1 - ctx_index) * span_rows])
    return (ctx_count, ctx_index, span_rows, span_starts)


def short_kernel(docs, window, taps, out):
    span_rows = out.shape[1]
    reach = window.shape[1] - span_rows
    tile = out.shape[2:]

    def outputs(number, _):
        half = number // (span_rows // ROWS)
        row = pl.multiple_of((number % (span_rows // ROWS)) * ROWS, ROWS)
        first_doc = docs[half, reach + row]
        last_doc = docs[half, reach + row + ROWS - 1]

        def sources(step, sums):
            begin = row + step * ROWS
            base = reach - step * ROWS

            def load():
                source = [window[half, begin + b] for b in range(ROWS)]
                weight = [taps[base + d] for d in range(2 * ROWS - 1)]
                return source, weight

            def plain(sums):
                source, weight = load()
                sums = list(sums)
                for b in range(ROWS):
                    for a in range(ROWS):
                        sums[a] = sums[a] + source[b] * weight[a - b + ROWS - 1]
                return tuple(sums)

            def masked(sums):
                source, weight = load()
                sums = list(sums)
                for b in range(ROWS):
                    doc = docs[half, begin + b]
                    for a in range(ROWS):
                        same = jnp.where(doc == docs[half, reach + row + a], 1.0, 0.0)
                        sums[a] = sums[a] + (source[b] * same) * weight[a - b + ROWS - 1]
                return tuple(sums)

            return lax.cond(docs[half, begin] == last_doc, plain, masked, sums)

        def outside(step, skipped):
            return skipped + jnp.where(docs[half, row + step * ROWS + ROWS - 1] < first_doc, 1, 0)

        steps = reach // ROWS + 1
        skip = lax.fori_loop(0, steps, outside, jnp.int32(0))
        zero = jnp.zeros(tile, jnp.float32)
        sums = lax.fori_loop(skip, steps, sources, (zero,) * ROWS)
        for a in range(ROWS):
            out[half, row + a] = sums[a]
        return 0

    lax.fori_loop(0, 2 * (span_rows // ROWS), outputs, 0)


def short_mix(product, mr_filter, doc_ids):
    shard_rows, channels = product.shape
    ctx_count, ctx_index, span_rows, span_starts = span_layout(shard_rows)
    tap_count = mr_filter.shape[0]
    reach = -(-tap_count // ROWS) * ROWS
    halves = product.reshape(2, span_rows, channels)
    tails = halves[:, span_rows - reach :]
    up = [(i, i + 1) for i in range(ctx_count - 1)]
    down = [(i + 1, i) for i in range(ctx_count - 1)]
    before_lower = lax.ppermute(tails[0], "ctx", up)
    before_upper = lax.ppermute(tails[1], "ctx", down)
    before_upper = jnp.where(ctx_index == ctx_count - 1, tails[0], before_upper)
    window = jnp.concatenate([jnp.stack([before_lower, before_upper]), halves], 1)
    tile = (channels // LANES, LANES)
    window = window.astype(jnp.float32).reshape((2, reach + span_rows) + tile)
    places = span_starts[:, None] - reach + jnp.arange(reach + span_rows)[None, :]
    docs = jnp.where(places >= 0, jnp.take(doc_ids, jnp.clip(places, 0, None)), -1)
    taps = jnp.pad(mr_filter, ((ROWS - 1, reach + ROWS - tap_count), (0, 0)))
    taps = taps.reshape((taps.shape[0],) + tile)
    mixed = pl.pallas_call(
        short_kernel,
        out_shape=jax.ShapeDtypeStruct((2, span_rows) + tile, jnp.float32),
        in_specs=[smem_spec, vmem_spec, vmem_spec],
        out_specs=vmem_spec,
        compiler_params=pltpu.CompilerParams(vmem_limit_bytes=VMEM_LIMIT),
        cost_estimate=pl.CostEstimate(
            flops=2 * shard_rows * tap_count * channels,
            bytes_accessed=8 * shard_rows * channels,
            transcendentals=0,
        ),
        name="short_mix",
    )(docs, window, taps)
    return mixed.reshape(shard_rows, channels)


def states_kernel(follows, factor, values, finals):
    span_rows, modes = (values.shape[1], factor.shape[0])
    tile = values.shape[2:]
    for half in range(2):

        def step(row, states):
            value, keep = (values[half, row], follows[half, row])
            return tuple(states[m] * (factor[m] * keep) + value for m in range(modes))

        zero = jnp.zeros(tile, jnp.float32)
        states = lax.fori_loop(0, span_rows, step, (zero,) * modes)
        for m in range(modes):
            finals[half, m] = states[m]


def long_kernel(follows, factor, residue, initial, values, out):
    span_rows, modes = (values.shape[1], factor.shape[0])
    for half in range(2):

        def step(row, states):
            value, keep = (values[half, row], follows[half, row])
            states = tuple(states[m] * (factor[m] * keep) + value for m in range(modes))
            terms = [states[m] * residue[m] for m in range(modes)]
            while len(terms) > 1:
                pairs = [terms[k] + terms[k + 1] for k in range(0, len(terms) - 1, 2)]
                terms = pairs + terms[len(terms) - len(terms) % 2 :]
            out[half, row] = terms[0]
            return states

        lax.fori_loop(0, span_rows, step, tuple(initial[half, m] for m in range(modes)))


def long_tables(shard_rows, li_decay, li_residue, doc_ids):
    ctx_count, ctx_index, span_rows, span_starts = span_layout(shard_rows)
    modes, channels = li_decay.shape
    tile = (channels // LANES, LANES)
    decay = li_decay.reshape((modes,) + tile)
    residue = li_residue.reshape((modes,) + tile)
    factor = jnp.exp(-decay)
    places = span_starts[:, None] + jnp.arange(span_rows)[None, :]
    earlier = jnp.take(doc_ids, jnp.clip(places - 1, 0, None))
    follows = ((places > 0) & (jnp.take(doc_ids, places) == earlier)).astype(jnp.float32)
    source = (ctx_index - jnp.arange(ctx_count)) % ctx_count
    block = jnp.stack([source, 2 * ctx_count - 1 - source], 1)
    last = (block + 1) * span_rows - 1
    gap = span_starts - 1 - last[:, :, None]
    keep = (gap >= 0) & (jnp.take(doc_ids, last)[:, :, None] == earlier[:, 0])
    distance = jnp.where(keep, gap, 0).astype(jnp.float32)[..., None, None, None]
    weights = jnp.exp(-decay * distance) * keep.astype(jnp.float32)[..., None, None, None]
    return (factor, residue, follows, weights)


def long_mix(product, tables):
    shard_rows, channels = product.shape
    ctx_count, ctx_index, span_rows, span_starts = span_layout(shard_rows)
    factor, residue, follows, weights = tables
    modes = factor.shape[0]
    tile = (channels // LANES, LANES)
    values = product.astype(jnp.float32).reshape((2, span_rows) + tile)
    params = pltpu.CompilerParams(vmem_limit_bytes=VMEM_LIMIT)
    flops = 2 * shard_rows * modes * channels
    finals = pl.pallas_call(
        states_kernel,
        out_shape=jax.ShapeDtypeStruct((2, modes) + tile, jnp.float32),
        in_specs=[smem_spec, vmem_spec, vmem_spec],
        out_specs=vmem_spec,
        compiler_params=params,
        cost_estimate=pl.CostEstimate(
            flops=flops, bytes_accessed=4 * shard_rows * channels, transcendentals=0
        ),
        name="block_states",
    )(follows, factor, values)
    initial = jnp.zeros((2, modes) + tile, jnp.float32)
    for shift in range(ctx_count):
        states = finals
        if shift:
            ring = [(i, (i + shift) % ctx_count) for i in range(ctx_count)]
            states = lax.ppermute(finals, "ctx", ring)
        for part in range(2):
            initial = initial + weights[shift, part] * states[part][None]
    mixed = pl.pallas_call(
        long_kernel,
        out_shape=jax.ShapeDtypeStruct((2, span_rows) + tile, jnp.float32),
        in_specs=[smem_spec] + [vmem_spec] * 4,
        out_specs=vmem_spec,
        compiler_params=params,
        cost_estimate=pl.CostEstimate(
            flops=2 * flops, bytes_accessed=8 * shard_rows * channels, transcendentals=0
        ),
        name="long_mix",
    )(follows, factor, residue, initial, values)
    return mixed.reshape(shard_rows, channels)


def body(
    tokens,
    mr_gain,
    mr_inproj,
    mr_outproj,
    mr_filter,
    li_gain,
    li_inproj,
    li_outproj,
    li_decay,
    li_residue,
    doc_ids,
):
    mr_in = lax.all_gather(mr_inproj, "ctx", axis=0, tiled=True)
    mr_out = lax.all_gather(mr_outproj, "ctx", axis=1, tiled=True)
    li_in = lax.all_gather(li_inproj, "ctx", axis=0, tiled=True)
    li_out = lax.all_gather(li_outproj, "ctx", axis=1, tiled=True)
    shard_rows = tokens.shape[0]
    early = long_tables(shard_rows, li_decay, li_residue, doc_ids)
    streams = [tokens[: shard_rows // 2], tokens[shard_rows // 2 :]]
    query, product, tables = features_in([tokens], mr_gain, mr_in, early)
    streams = features_out(streams, query, short_mix(product, mr_filter, doc_ids), mr_out)
    query, product, _ = features_in(streams, li_gain, li_in, None)
    streams = features_out(streams, query, long_mix(product, tables), li_out)
    return jnp.concatenate(streams, axis=0)


def solution(mesh):
    in_specs = (
        P("ctx", "ch"),
        P(),
        P("ctx", None, "ch"),
        P("ch", "ctx"),
        P(None, "ch"),
        P(),
        P("ctx", None, "ch"),
        P("ch", "ctx"),
        P(None, "ch"),
        P(None, "ch"),
        P(),
    )
    out_specs = P("ctx", "ch")
    return jax.shard_map(body, mesh=mesh, in_specs=in_specs, out_specs=out_specs, check_vma=False)
```

```python
import functools

import jax
import jax.numpy as jnp
from jax import lax
from jax.experimental import pallas as pl
from jax.experimental.pallas import tpu as pltpu
from jax.sharding import PartitionSpec as P

LANES = 128
ROWS = 8
VMEM_LIMIT = 40 * 1024 * 1024
vmem_spec = pl.BlockSpec(memory_space=pltpu.VMEM)
smem_spec = pl.BlockSpec(memory_space=pltpu.SMEM)


def gather_channels(stream):
    count, index = (lax.axis_size("ch"), lax.axis_index("ch"))
    channels = stream.shape[1]
    from_left, from_right = ([stream], [stream])
    for hop in range(1, count):
        up = [(i, i + 1) for i in range(hop - 1, count - 1)]
        down = [(i, i - 1) for i in range(1, count - hop + 1)]
        from_left.append(lax.ppermute(from_left[-1], "ch", up))
        from_right.append(lax.ppermute(from_right[-1], "ch", down))
    line = jnp.concatenate(from_left[:0:-1] + [stream] + from_right[1:], axis=1)
    return lax.dynamic_slice_in_dim(line, (count - 1 - index) * channels, count * channels, 1)


def scatter_channels(terms, streams):
    count, index = (lax.axis_size("ch"), lax.axis_index("ch"))
    rows, channels = streams[0].shape
    parts = range(len(streams))

    def block(part, number):
        begin = jnp.clip(number, 0, count - 1) * channels
        own = terms[part * rows : (part + 1) * rows]
        return lax.dynamic_slice_in_dim(own, begin, channels, 1).astype(jnp.float32)

    right, left = ([None for _ in parts], [None for _ in parts])
    for far in range(count - 1, 0, -1):
        up = [(i, i + 1) for i in range(count - far)]
        down = [(i, i - 1) for i in range(far, count)]
        for part in parts:
            rightward, leftward = (block(part, index + far), block(part, index - far))
            if right[part] is not None:
                rightward = rightward + right[part].astype(jnp.float32)
                leftward = leftward + left[part].astype(jnp.float32)
            right[part] = lax.ppermute(rightward.astype(jnp.bfloat16), "ch", up)
            left[part] = lax.ppermute(leftward.astype(jnp.bfloat16), "ch", down)
    summed = []
    for part in parts:
        total = block(part, index) + streams[part].astype(jnp.float32)
        total = total + right[part].astype(jnp.float32) + left[part].astype(jnp.float32)
        summed.append(total.astype(jnp.bfloat16))
    return summed


def features_in(streams, gain, piece, early):
    whole = jnp.concatenate([gather_channels(part) for part in streams], axis=0)
    floats = whole.astype(jnp.float32)
    scaled = lax.rsqrt(jnp.mean(floats * floats, axis=1, keepdims=True) + 1e-06)
    if early is not None:
        scaled, early = lax.optimization_barrier((scaled, early))
    normed = (floats * scaled * gain[None, :]).astype(jnp.bfloat16)
    channels = piece.shape[2]
    flat = piece.reshape(piece.shape[0], 3 * channels)
    joined = jnp.dot(normed, flat, preferred_element_type=jnp.float32).astype(jnp.bfloat16)
    product = (
        joined[:, channels : 2 * channels].astype(jnp.float32)
        * joined[:, 2 * channels :].astype(jnp.float32)
    ).astype(jnp.bfloat16)
    return (joined[:, :channels], product, early)


def features_out(streams, query, mixed, piece):
    gated = (query.astype(jnp.float32) * mixed).astype(jnp.bfloat16)
    terms = jnp.dot(gated, piece, preferred_element_type=jnp.float32).astype(jnp.bfloat16)
    return scatter_channels(terms, streams)


def span_layout(shard_rows):
    ctx_count = lax.axis_size("ctx")
    ctx_index = lax.axis_index("ctx")
    span_rows = shard_rows // 2
    span_starts = jnp.stack([ctx_index * span_rows, (2 * ctx_count - 1 - ctx_index) * span_rows])
    return (ctx_count, ctx_index, span_rows, span_starts)


def short_kernel(docs, window, taps, out):
    span_rows = out.shape[1]
    reach = window.shape[1] - span_rows
    tile = out.shape[2:]

    def outputs(number, _):
        half = number // (span_rows // ROWS)
        row = pl.multiple_of((number % (span_rows // ROWS)) * ROWS, ROWS)
        first_doc = docs[half, reach + row]
        last_doc = docs[half, reach + row + ROWS - 1]

        def sources(whole, step, sums):
            begin = row + step * ROWS
            base = reach - step * ROWS

            def load():
                source = [window[half, begin + b] for b in range(ROWS)]
                weight = [taps[base + d] for d in range(2 * ROWS - 1)]
                return source, weight

            def plain(sums):
                source, weight = load()
                sums = list(sums)
                for b in range(ROWS):
                    for a in range(ROWS):
                        sums[a] = sums[a] + source[b] * weight[a - b + ROWS - 1]
                return tuple(sums)

            def masked(sums):
                source, weight = load()
                sums = list(sums)
                for b in range(ROWS):
                    doc = docs[half, begin + b]
                    for a in range(ROWS):
                        same = jnp.where(doc == docs[half, reach + row + a], 1.0, 0.0)
                        sums[a] = sums[a] + (source[b] * same) * weight[a - b + ROWS - 1]
                return tuple(sums)

            return plain(sums) if whole else masked(sums)

        def outside(step, counts):
            begin = row + step * ROWS
            skipped = counts[0] + jnp.where(docs[half, begin + ROWS - 1] < first_doc, 1, 0)
            return skipped, counts[1] + jnp.where(docs[half, begin] == last_doc, 0, 1)

        steps = reach // ROWS + 1
        skip, mixed = lax.fori_loop(0, steps, outside, (jnp.int32(0), jnp.int32(0)))
        sums = (jnp.zeros(tile, jnp.float32),) * ROWS
        sums = lax.fori_loop(skip, mixed, functools.partial(sources, False), sums)
        sums = lax.fori_loop(mixed, steps, functools.partial(sources, True), sums)
        for a in range(ROWS):
            out[half, row + a] = sums[a]
        return 0

    lax.fori_loop(0, 2 * (span_rows // ROWS), outputs, 0)


def short_mix(product, mr_filter, doc_ids):
    shard_rows, channels = product.shape
    ctx_count, ctx_index, span_rows, span_starts = span_layout(shard_rows)
    tap_count = mr_filter.shape[0]
    reach = -(-tap_count // ROWS) * ROWS
    halves = product.reshape(2, span_rows, channels)
    tails = halves[:, span_rows - reach :]
    up = [(i, i + 1) for i in range(ctx_count - 1)]
    down = [(i + 1, i) for i in range(ctx_count - 1)]
    before_lower = lax.ppermute(tails[0], "ctx", up)
    before_upper = lax.ppermute(tails[1], "ctx", down)
    before_upper = jnp.where(ctx_index == ctx_count - 1, tails[0], before_upper)
    window = jnp.concatenate([jnp.stack([before_lower, before_upper]), halves], 1)
    tile = (channels // LANES, LANES)
    window = window.astype(jnp.float32).reshape((2, reach + span_rows) + tile)
    places = span_starts[:, None] - reach + jnp.arange(reach + span_rows)[None, :]
    docs = jnp.where(places >= 0, jnp.take(doc_ids, jnp.clip(places, 0, None)), -1)
    taps = jnp.pad(mr_filter, ((ROWS - 1, reach + ROWS - tap_count), (0, 0)))
    taps = taps.reshape((taps.shape[0],) + tile)
    mixed = pl.pallas_call(
        short_kernel,
        out_shape=jax.ShapeDtypeStruct((2, span_rows) + tile, jnp.float32),
        in_specs=[smem_spec, vmem_spec, vmem_spec],
        out_specs=vmem_spec,
        compiler_params=pltpu.CompilerParams(vmem_limit_bytes=VMEM_LIMIT),
        cost_estimate=pl.CostEstimate(
            flops=2 * shard_rows * tap_count * channels,
            bytes_accessed=8 * shard_rows * channels,
            transcendentals=0,
        ),
        name="short_mix",
    )(docs, window, taps)
    return mixed.reshape(shard_rows, channels)


def states_kernel(follows, factor, values, finals):
    span_rows, modes = (values.shape[1], factor.shape[0])
    tile = values.shape[2:]
    for half in range(2):

        def step(row, states):
            value, keep = (values[half, row], follows[half, row])
            return tuple(states[m] * (factor[m] * keep) + value for m in range(modes))

        zero = jnp.zeros(tile, jnp.float32)
        states = lax.fori_loop(0, span_rows, step, (zero,) * modes)
        for m in range(modes):
            finals[half, m] = states[m]


def long_kernel(follows, factor, residue, initial, values, out):
    span_rows, modes = (values.shape[1], factor.shape[0])
    for half in range(2):

        def step(row, states):
            value, keep = (values[half, row], follows[half, row])
            states = tuple(states[m] * (factor[m] * keep) + value for m in range(modes))
            terms = [states[m] * residue[m] for m in range(modes)]
            while len(terms) > 1:
                pairs = [terms[k] + terms[k + 1] for k in range(0, len(terms) - 1, 2)]
                terms = pairs + terms[len(terms) - len(terms) % 2 :]
            out[half, row] = terms[0]
            return states

        lax.fori_loop(0, span_rows, step, tuple(initial[half, m] for m in range(modes)))


def long_tables(shard_rows, li_decay, li_residue, doc_ids):
    ctx_count, ctx_index, span_rows, span_starts = span_layout(shard_rows)
    modes, channels = li_decay.shape
    tile = (channels // LANES, LANES)
    decay = li_decay.reshape((modes,) + tile)
    residue = li_residue.reshape((modes,) + tile)
    factor = jnp.exp(-decay)
    places = span_starts[:, None] + jnp.arange(span_rows)[None, :]
    earlier = jnp.take(doc_ids, jnp.clip(places - 1, 0, None))
    follows = ((places > 0) & (jnp.take(doc_ids, places) == earlier)).astype(jnp.float32)
    source = (ctx_index - jnp.arange(ctx_count)) % ctx_count
    block = jnp.stack([source, 2 * ctx_count - 1 - source], 1)
    last = (block + 1) * span_rows - 1
    gap = span_starts - 1 - last[:, :, None]
    keep = (gap >= 0) & (jnp.take(doc_ids, last)[:, :, None] == earlier[:, 0])
    distance = jnp.where(keep, gap, 0).astype(jnp.float32)[..., None, None, None]
    weights = jnp.exp(-decay * distance) * keep.astype(jnp.float32)[..., None, None, None]
    return (factor, residue, follows, weights)


def long_mix(product, tables):
    shard_rows, channels = product.shape
    ctx_count, ctx_index, span_rows, span_starts = span_layout(shard_rows)
    factor, residue, follows, weights = tables
    modes = factor.shape[0]
    tile = (channels // LANES, LANES)
    values = product.astype(jnp.float32).reshape((2, span_rows) + tile)
    params = pltpu.CompilerParams(vmem_limit_bytes=VMEM_LIMIT)
    flops = 2 * shard_rows * modes * channels
    finals = pl.pallas_call(
        states_kernel,
        out_shape=jax.ShapeDtypeStruct((2, modes) + tile, jnp.float32),
        in_specs=[smem_spec, vmem_spec, vmem_spec],
        out_specs=vmem_spec,
        compiler_params=params,
        cost_estimate=pl.CostEstimate(
            flops=flops, bytes_accessed=4 * shard_rows * channels, transcendentals=0
        ),
        name="block_states",
    )(follows, factor, values)
    initial = jnp.zeros((2, modes) + tile, jnp.float32)
    for shift in range(ctx_count):
        states = finals
        if shift:
            ring = [(i, (i + shift) % ctx_count) for i in range(ctx_count)]
            states = lax.ppermute(finals, "ctx", ring)
        for part in range(2):
            initial = initial + weights[shift, part] * states[part][None]
    mixed = pl.pallas_call(
        long_kernel,
        out_shape=jax.ShapeDtypeStruct((2, span_rows) + tile, jnp.float32),
        in_specs=[smem_spec] + [vmem_spec] * 4,
        out_specs=vmem_spec,
        compiler_params=params,
        cost_estimate=pl.CostEstimate(
            flops=2 * flops, bytes_accessed=8 * shard_rows * channels, transcendentals=0
        ),
        name="long_mix",
    )(follows, factor, residue, initial, values)
    return mixed.reshape(shard_rows, channels)


def body(
    tokens,
    mr_gain,
    mr_inproj,
    mr_outproj,
    mr_filter,
    li_gain,
    li_inproj,
    li_outproj,
    li_decay,
    li_residue,
    doc_ids,
):
    mr_in = lax.all_gather(mr_inproj, "ctx", axis=0, tiled=True)
    mr_out = lax.all_gather(mr_outproj, "ctx", axis=1, tiled=True)
    li_in = lax.all_gather(li_inproj, "ctx", axis=0, tiled=True)
    li_out = lax.all_gather(li_outproj, "ctx", axis=1, tiled=True)
    shard_rows = tokens.shape[0]
    early = long_tables(shard_rows, li_decay, li_residue, doc_ids)
    streams = [tokens[: shard_rows // 2], tokens[shard_rows // 2 :]]
    query, product, tables = features_in([tokens], mr_gain, mr_in, early)
    streams = features_out(streams, query, short_mix(product, mr_filter, doc_ids), mr_out)
    query, product, _ = features_in(streams, li_gain, li_in, None)
    streams = features_out(streams, query, long_mix(product, tables), li_out)
    return jnp.concatenate(streams, axis=0)


def solution(mesh):
    in_specs = (
        P("ctx", "ch"),
        P(),
        P("ctx", None, "ch"),
        P("ch", "ctx"),
        P(None, "ch"),
        P(),
        P("ctx", None, "ch"),
        P("ch", "ctx"),
        P(None, "ch"),
        P(None, "ch"),
        P(),
    )
    out_specs = P("ctx", "ch")
    return jax.shard_map(body, mesh=mesh, in_specs=in_specs, out_specs=out_specs, check_vma=False)
```
